768 devices in a mesh: own: 12 (over z), neg: 32 (over x, y), rep: 2 (over core).
Axes of the slice: x: 4, y: 8, z: 12, core: 2. Of those that a mesh axis runs over, the one named last changes fastest.
Arguments:
- user_vec: bfloat16 [24, 8192, 256], P(('own', 'rep'), 'neg'), may hold values from -6 to 6
- item_rows: bfloat16 [24, 8192, 256], P(('own', 'rep'), 'neg'), may hold values from -6 to 6
- w_item: bfloat16 [256, 256], replicated, may hold values from -0.375 to 0.375
- item_count: int32 [24, 8192], P(('own', 'rep'), 'neg'), may hold values from 64 to 4095
- item_owner: int32 [24, 8192, 1], P(('own', 'rep'), 'neg'), may hold values from 0 to 12; in each aligned block of 256 rows (0 to 255, 256 to 511, ..., all dimensions but the last counted through in order) at most 56 rows name the same one
- hot_row: int32 [24, 8192], P(('own', 'rep'), 'neg'), may hold values from 0 to 511
- cold_offset: int32 [24, 8192], P(('own', 'rep'), 'neg'), may hold values from 0 to 511
- hot_table: float32 [512, 256], replicated, may hold values from -6 to 6
- hot_accum: float32 [512, 256], replicated, may hold values from 0.01 to 1
- cold_table: float32 [12, 32768, 256], P('own', ('neg', 'rep')), may hold values from -6 to 6
- cold_accum: float32 [12, 32768, 256], P('own', ('neg', 'rep')), may hold values from 0.01 to 1
Outputs:
- user_grad: bfloat16 [24, 8192, 256], P(('own', 'rep'), 'neg')
- w_grad: float32 [256, 256], replicated
- hot_table_new: float32 [512, 256], replicated
- hot_accum_new: float32 [512, 256], replicated
- cold_table_new: float32 [12, 32768, 256], P('own', ('neg', 'rep'))
- cold_accum_new: float32 [12, 32768, 256], P('own', ('neg', 'rep'))
The draws below stay inside these ranges and needn't reach their ends.
Inputs may be any that keep to these rules, and one draw needn't show every extreme that they name: `item_owner`: 12 marks a pair whose item is hot; a smaller value names the owner of its cold row. Among the 256 pairs of one device no value occurs more than 56 times, and some value occurs exactly 56 times.
All inputs are finite; a program needn't handle non-finite values.
Results may differ from the reference program's by a relative error of at most 0.0041.
The reference program's roundings to bfloat16 on the way (of `user_unit`, `item_unit`, `score_grad`, `item_vec_grad` and `row_grad`) count: a program that leaves them out, or rounds other values in their place, can miss the bound.
Values may be sent and summed in bfloat16 or wider, within the bound.
No kernel may reach another device: no remote copies, remote signals or barrier semaphores. Data moves between devices by JAX's collectives and lax.ppermute only.
A program may use at most 64 MiB of HBM per device.

```python
import math
import jax
import jax.numpy as jnp
import numpy as np
from jax import lax

E = 256
B = 256
ROWS_DEV = 512
HOT = 512
CAP = 56
GROUPS = 24
GROUP_PAIRS = 8192
COLS = 32768
N_OWN = 12
N_REP = 2


def set_ends(result, own_key, low, high):
    spot = [jax.random.randint(jax.random.fold_in(own_key, axis), (), 0, length) for axis, length in enumerate(result.shape)]
    main_axis = result.shape.index(max(result.shape))
    next_to = spot[:main_axis] + [(spot[main_axis] + 1) % result.shape[main_axis]] + spot[main_axis + 1:]
    return result.at[tuple(spot)].set(low).at[tuple(next_to)].set(high)


def shard_levels(key, extent, split, smallest, largest):
    factor_of = 1.0
    for axis_at, shards_of in split:
        draws = jax.random.uniform(jax.random.fold_in(jax.random.fold_in(key, 6), axis_at), (shards_of,), jnp.float32, smallest / len(split), largest / len(split))
        factor_of = factor_of * jnp.repeat(jnp.exp(draws), extent[axis_at] // shards_of).reshape((-1,) + (1,) * (len(extent) - 1 - axis_at))
    return factor_of


def shared_out(own_key, own, number, rows, number_of, top, reach, lean):
    ranking = jax.random.permutation(own_key, number_of)
    packed, common = portions_of(number_of, rows * top, reach, lean, True), portions_of(number_of, rows * top, reach, lean, False)
    places = jnp.arange(number_of)

    def named(lengths, rotation):
        used = int((lengths > 0).sum())
        fixed = max(1, used // 4)
        moved = fixed + (places - fixed + rotation * (used - fixed)) % max(1, number_of - fixed)
        return jnp.zeros((number_of,), jnp.int32).at[ranking[jnp.where(places < fixed, places, moved)]].set(jnp.asarray(lengths, jnp.int32))

    lengths = jnp.where(number % 4 == 0, named(packed, number // 4), named(common, number - number // 4 - 1))
    mixed = jax.random.permutation(jax.random.fold_in(own, 3), number_of)
    source_of, sink = mixed[0:number_of // 2 * 2:2], mixed[1:number_of // 2 * 2:2]
    room = jnp.minimum(lengths[source_of] - 1, reach - lengths[sink]) // 2
    room = jnp.where((source_of == ranking[0]) | (sink == ranking[0]) | (lengths[sink] == 0), 0, jnp.maximum(room, 0))
    moved = jax.random.randint(jax.random.fold_in(own, 4), (number_of // 2,), 0, 1 << 20) % (room + 1)
    lengths = lengths.at[source_of].add(-moved).at[sink].add(moved)
    labels = jnp.searchsorted(jnp.cumsum(lengths), jnp.arange(rows * top), side="right").astype(jnp.int32)
    table = labels.reshape(top, rows).T
    table = table[jax.random.permutation(jax.random.fold_in(own, 1), rows)]
    rotation = jax.random.randint(jax.random.fold_in(own, 2), (rows, 1), 0, top)
    return jnp.take_along_axis(table, (jnp.arange(top)[None, :] + rotation) % top, axis=1)


def portions_of(amount, total, bound, skew, full):
    portions = [(1 << 20) // math.isqrt(grade ** skew) + 1 for grade in range(1, amount + 1)]
    largest = bound if full else min(bound, max(-(-total // amount), total * portions[0] // sum(portions)))
    least = 1 if total - largest >= amount - 1 else 0
    holding, rest = [largest] + [least] * (amount - 1), total - largest - least * (amount - 1)
    while rest > 0:
        candidates = [i for i in range(1, amount) if holding[i] < largest] or [i for i in range(1, amount) if holding[i] < bound]
        mass, left = sum([portions[i] for i in candidates]), rest
        for i in candidates:
            extra = min(bound - holding[i], max(1, left * portions[i] // mass), rest)
            holding[i] = holding[i] + extra
            rest = rest - extra
    return np.array(holding)


def bell_draw(stream_key, dims, width, bound, cuts=(), kind=jnp.bfloat16):
    values = jax.random.normal(stream_key, dims, jnp.float32) * width
    if len(cuts) > 0:
        values = shard_levels(stream_key, dims, cuts, -0.22, 0.18) * values
    return jnp.clip(values, min=-bound, max=bound).astype(kind)


def setup_inputs(seed: int = 0) -> dict:
    key_list = jax.random.split(jax.random.key(seed), 12)
    user_vec = bell_draw(key_list[0], (GROUPS, GROUP_PAIRS, E), 1.0, 6.0, ((0, 24), (1, 32)))
    item_rows = bell_draw(key_list[1], (GROUPS, GROUP_PAIRS, E), 1.0, 6.0, ((0, 24), (1, 32)))
    w_item = bell_draw(key_list[2], (E, E), E ** -0.5, 0.375)
    item_count = set_ends(jax.random.randint(key_list[3], (GROUPS, GROUP_PAIRS), 64, 4096), jax.random.fold_in(key_list[3], 1), 64, 4095).astype(jnp.int32)
    item_owner_keys = jax.random.split(jax.random.fold_in(key_list[4], 1), GROUPS * GROUP_PAIRS // B)
    item_owner_turns = jax.random.permutation(jax.random.fold_in(key_list[4], 3), GROUPS * GROUP_PAIRS // B)
    item_owner = jax.vmap(lambda own, number: shared_out(jax.random.fold_in(key_list[4], 2), own, number, B, N_OWN + 1, 1, CAP, 2))(item_owner_keys, item_owner_turns).reshape((GROUPS, GROUP_PAIRS, 1))
    hot_row = set_ends(jax.random.randint(key_list[5], (GROUPS, GROUP_PAIRS), 0, HOT), jax.random.fold_in(key_list[5], 1), 0, HOT - 1).astype(jnp.int32)
    cold_offset = set_ends(jax.random.randint(key_list[6], (GROUPS, GROUP_PAIRS), 0, ROWS_DEV), jax.random.fold_in(key_list[6], 1), 0, ROWS_DEV - 1).astype(jnp.int32)
    hot_table = bell_draw(key_list[7], (HOT, E), 1.0, 6.0, (), jnp.float32)
    hot_accum = jnp.clip(jnp.exp(jax.random.uniform(key_list[8], (HOT, E), jnp.float32, math.log(0.01), math.log(1.0))), 0.01, 1.0)
    cold_table = bell_draw(key_list[9], (N_OWN, COLS, E), 1.0, 6.0, ((0, 12), (1, 64)), jnp.float32)
    cold_accum = jnp.clip(jnp.exp(math.log(1.0) - 4.6051702 * jax.random.uniform(key_list[10], (N_OWN, COLS, E), jnp.float32) ** shard_levels(key_list[10], (N_OWN, COLS, E), ((0, 12), (1, 64)), -0.2, 0.2)), 0.01, 1.0)
    return {"user_vec": user_vec, "item_rows": item_rows, "w_item": w_item, "item_count": item_count, "item_owner": item_owner, "hot_row": hot_row, "cold_offset": cold_offset, "hot_table": hot_table, "hot_accum": hot_accum, "cold_table": cold_table, "cold_accum": cold_accum}


score_scale = 20.0
learn_rate = 0.1
norm_eps = 1e-06

def normalize(values):
    factor = lax.rsqrt(lax.optimization_barrier(jnp.sum(values * values, axis=-1, keepdims=True)) + norm_eps)
    return (values * factor, factor)

def norm_backward(values, factor, upstream):
    inner = lax.optimization_barrier(jnp.sum(values * upstream, axis=-1, keepdims=True))
    return factor * upstream - factor * factor * factor * values * inner

def adagrad(table, accum, grads):
    accum_new = accum + grads * grads
    return (table - learn_rate * grads * lax.rsqrt(accum_new), accum_new)

def reference(user_vec, item_rows, w_item, item_count, item_owner, hot_row, cold_offset, hot_table, hot_accum, cold_table, cold_accum):

    def group_backward(inputs):
        user_block, item_block, count_block = inputs
        user_float = user_block.astype(jnp.float32)
        user_norm, user_factor = normalize(user_float)
        user_unit = user_norm.astype(jnp.bfloat16)
        item_vec = jnp.dot(item_block, w_item, preferred_element_type=jnp.float32)
        item_norm, item_factor = normalize(item_vec)
        item_unit = item_norm.astype(jnp.bfloat16)
        logits = score_scale * jnp.dot(user_unit, item_unit.T, preferred_element_type=jnp.float32)
        logits = logits - jnp.log(count_block.astype(jnp.float32))[None, :]
        totals = jnp.log(lax.optimization_barrier(jnp.sum(jnp.exp(logits), axis=1)))
        positive = jnp.eye(GROUP_PAIRS, dtype=jnp.float32)
        score_grad = (jnp.exp(logits - totals[:, None]) - positive).astype(jnp.bfloat16)
        user_unit_grad = score_scale * jnp.dot(score_grad, item_unit, preferred_element_type=jnp.float32)
        item_unit_grad = score_scale * jnp.dot(score_grad.T, user_unit, preferred_element_type=jnp.float32)
        user_grad = norm_backward(user_float, user_factor, user_unit_grad).astype(jnp.bfloat16)
        item_vec_grad = norm_backward(item_vec, item_factor, item_unit_grad).astype(jnp.bfloat16)
        return (user_grad, item_vec_grad)
    user_grad, item_vec_grad = lax.map(group_backward, (user_vec, item_rows, item_count))
    flat_grad = item_vec_grad.reshape(-1, E)
    row_grad = jnp.dot(flat_grad, w_item.T, preferred_element_type=jnp.float32)
    row_grad = lax.optimization_barrier(row_grad.astype(jnp.bfloat16)).astype(jnp.float32)
    w_grad = jnp.dot(item_rows.reshape(-1, E).T, flat_grad, preferred_element_type=jnp.float32)
    owner_flat = item_owner[..., 0].reshape(-1).astype(jnp.int32)
    is_hot = owner_flat == N_OWN
    hot_index = jnp.where(is_hot, hot_row.reshape(-1).astype(jnp.int32), HOT).astype(jnp.int32)
    hot_grad = jnp.zeros((HOT, E), jnp.float32).at[hot_index].add(row_grad, mode='drop')
    hot_table_new, hot_accum_new = adagrad(hot_table, hot_accum, hot_grad)
    group_index = jnp.arange(GROUPS, dtype=jnp.int32)[:, None]
    pair_index = jnp.arange(GROUP_PAIRS, dtype=jnp.int32)[None, :]
    column = (pair_index // B * N_REP + group_index % N_REP) * ROWS_DEV + cold_offset.astype(jnp.int32)
    column = column.reshape(-1).astype(jnp.int32)
    cold_grad = jnp.zeros((N_OWN, COLS, E), jnp.float32).at[owner_flat, column].add(row_grad, mode='drop')
    cold_table_new, cold_accum_new = adagrad(cold_table, cold_accum, cold_grad)
    return (user_grad, w_grad, hot_table_new, hot_accum_new, cold_table_new, cold_accum_new)
```

```python
import jax
import jax.numpy as jnp
from jax import lax
from jax.sharding import Mesh, PartitionSpec as P

CAP = 56
NX = 4
SLOTS = 64

score_scale = 20.0
learn_rate = 0.1
norm_eps = 1e-06

bf16 = jnp.bfloat16
f32 = jnp.float32
i32 = jnp.int32


def normalize(values):
    factor = lax.rsqrt(jnp.sum(values * values, axis=-1, keepdims=True) + norm_eps)
    return (values * factor, factor)


def norm_backward(values, factor, upstream):
    inner = jnp.sum(values * upstream, axis=-1, keepdims=True)
    return factor * upstream - factor * factor * factor * values * inner


def adagrad(table, accum, grads):
    accum_new = accum + grads * grads
    return (table - learn_rate * grads * lax.rsqrt(accum_new), accum_new)


def contract_first(left, right):
    return lax.dot_general(
        left, right, (((0,), (0,)), ((), ())), preferred_element_type=f32
    )


def contract_last(left, right):
    return lax.dot_general(
        left, right, (((1,), (1,)), ((), ())), preferred_element_type=f32
    )


def exchange(blocks, axis):
    return lax.all_to_all(blocks, axis, split_axis=0, concat_axis=0, tiled=True)


def spread(block, axis):
    count = lax.axis_size(axis)
    return exchange(jnp.broadcast_to(block[None], (count,) + block.shape), axis)


def reduce_blocks(blocks, axis):
    me = lax.axis_index(axis)
    got = exchange(blocks.astype(bf16), axis)
    own = lax.dynamic_index_in_dim(blocks, me, 0, keepdims=False)
    others = jnp.arange(blocks.shape[0], dtype=i32)[:, None, None] != me
    return own + jnp.sum(jnp.where(others, got.astype(f32), 0.0), axis=0)


def on_device(
    user_vec,
    item_rows,
    w_item,
    item_count,
    item_owner,
    hot_row,
    cold_offset,
    hot_table,
    hot_accum,
    cold_table,
    cold_accum,
):
    owners = lax.axis_size("own")
    ny = lax.axis_size("ny")
    nx = lax.axis_size("nx")
    user_float = user_vec[0].astype(f32)
    item_block = item_rows[0]
    batch_rows, width = item_block.shape
    with jax.named_scope("users_along_y"):
        user_norm, user_factor = normalize(user_float)
        user_unit = user_norm.astype(bf16)
        users = spread(user_unit, "ny").reshape(ny * batch_rows, width)
    with jax.named_scope("items_along_x"):
        item_vec = jnp.dot(item_block, w_item, preferred_element_type=f32)
        item_norm, item_factor = normalize(item_vec)
        item_unit = item_norm.astype(bf16)
        counts = item_count[0]
        count_rows = jnp.stack([counts // 256, counts % 256]).astype(bf16)
        packed = jnp.concatenate(
            [item_unit, jnp.pad(count_rows, ((0, 14), (0, 0)))], axis=0
        )
        got_items = spread(packed, "nx")
        items = got_items[:, :batch_rows].reshape(nx * batch_rows, width)
        got_counts = got_items[:, batch_rows : batch_rows + 2].astype(f32)
        all_counts = (got_counts[:, 0] * 256.0 + got_counts[:, 1]).reshape(-1)
    with jax.named_scope("scores"):
        logits = score_scale * contract_last(users, items)
        logits = logits - jnp.log(all_counts)[None, :]
        part_sums = jnp.sum(jnp.exp(logits), axis=1)
    with jax.named_scope("sums_along_y"):
        totals = jnp.log(jnp.sum(spread(part_sums.reshape(-1, 128), "ny"), axis=0)).reshape(-1)
    with jax.named_scope("score_grad"):
        row = jnp.arange(ny * batch_rows, dtype=i32) - lax.axis_index("ny") * batch_rows
        col = jnp.arange(nx * batch_rows, dtype=i32) - lax.axis_index("nx") * batch_rows
        row = jnp.where((row >= 0) & (row < batch_rows), row, -(1 << 20))
        positive = row[:, None] == col[None, :]
        score_grad = (
            jnp.exp(logits - totals[:, None]) - positive.astype(f32)
        ).astype(bf16)
    with jax.named_scope("item_grad"):
        item_part = score_scale * contract_first(score_grad, users)
        item_unit_grad = reduce_blocks(item_part.reshape(nx, batch_rows, width), "nx")
        item_vec_grad = norm_backward(item_vec, item_factor, item_unit_grad).astype(bf16)
        row_grad = contract_last(item_vec_grad, w_item).astype(bf16)
    with jax.named_scope("user_grad"):
        user_part = score_scale * jnp.dot(score_grad, items, preferred_element_type=f32)
        user_unit_grad = reduce_blocks(user_part.reshape(ny, batch_rows, width), "ny")
        user_grad = norm_backward(user_float, user_factor, user_unit_grad).astype(bf16)
    owner_id = item_owner[0, :, 0]
    with jax.named_scope("hot_and_w"):
        w_local = contract_first(item_block, item_vec_grad)
        hot_count = hot_table.shape[0]
        hot_match = (hot_row[0][:, None] == jnp.arange(hot_count, dtype=i32)[None, :]) & (
            owner_id == owners
        )[:, None]
        hot_local = contract_first(hot_match.astype(bf16), row_grad)
        local = jnp.concatenate([hot_local, w_local], axis=0)
        rows = local.shape[0]
        half = width // 2
        chip = jnp.sum(exchange(jnp.stack([local[:, :half], local[:, half:]]), "rep"), axis=0)
        plane = jnp.sum(
            exchange(chip.reshape(nx * ny, rows // (nx * ny), half), ("nx", "ny")), axis=0
        )
        total = jnp.sum(spread(plane, "own"), axis=0)
        mine = spread(total, ("nx", "ny")).reshape(rows, half)
        sides = spread(mine, "rep")
        summed = jnp.concatenate([sides[0], sides[1]], axis=1)
        hot_table_new, hot_accum_new = adagrad(hot_table, hot_accum, summed[:hot_count])
        w_grad = summed[hot_count:]
    with jax.named_scope("cold"):
        owner_hits = (owner_id[:, None] == jnp.arange(owners, dtype=i32)[None, :]).astype(bf16)
        place = jnp.arange(batch_rows, dtype=i32)
        earlier = (place[:, None] > place[None, :]).astype(bf16)
        before = jnp.dot(earlier, owner_hits, preferred_element_type=f32)
        slot = jnp.sum(before * owner_hits.astype(f32), axis=1).astype(i32)
        target = jnp.where(owner_id < owners, owner_id * SLOTS + slot, -1)
        placed = (
            jnp.arange(owners * SLOTS, dtype=i32)[:, None] == target[None, :]
        ).astype(bf16)
        mark = cold_offset[0] + 1
        slot_hits = (slot[:, None] == jnp.arange(SLOTS, dtype=i32)[None, :]).astype(bf16)
        high = contract_first(owner_hits * (mark // 256).astype(bf16)[:, None], slot_hits)
        low = contract_first(owner_hits * (mark % 256).astype(bf16)[:, None], slot_hits)
        marks = jnp.concatenate([high, low], axis=1).astype(bf16)
        marks = jnp.pad(marks[:, None, :], ((0, 0), (0, SLOTS - CAP - 1), (0, width - 2 * SLOTS)))
        send_rows = jnp.dot(placed, row_grad, preferred_element_type=f32).astype(bf16)
        send_rows = send_rows.reshape(owners, SLOTS, width)[:, :CAP]
        got = exchange(jnp.concatenate([send_rows, marks], axis=1), "own")
        got_marks = got[:, CAP].astype(f32)
        offsets = (got_marks[:, :SLOTS] * 256.0 + got_marks[:, SLOTS : 2 * SLOTS]).astype(i32) - 1
        local_rows = cold_table.shape[1]
        lands = (
            jnp.arange(local_rows, dtype=i32)[:, None] == offsets.reshape(-1)[None, :]
        ).astype(bf16)
        cold_grad = jnp.dot(
            lands, got.reshape(owners * SLOTS, width), preferred_element_type=f32
        )
        cold_table_new, cold_accum_new = adagrad(cold_table[0], cold_accum[0], cold_grad)
    return (
        user_grad[None],
        w_grad,
        hot_table_new,
        hot_accum_new,
        cold_table_new[None],
        cold_accum_new[None],
    )


def solution(mesh):
    owners, neg, rep = (mesh.shape[name] for name in ("own", "neg", "rep"))
    grid = Mesh(
        mesh.devices.reshape(owners, NX, neg // NX, rep), ("own", "nx", "ny", "rep")
    )
    group, pairs, blocks = ("own", "rep"), ("nx", "ny"), ("nx", "ny", "rep")
    return jax.shard_map(
        on_device,
        mesh=grid,
        in_specs=(
            P(group, pairs, None),
            P(group, pairs, None),
            P(),
            P(group, pairs),
            P(group, pairs, None),
            P(group, pairs),
            P(group, pairs),
            P(),
            P(),
            P("own", blocks, None),
            P("own", blocks, None),
        ),
        out_specs=(
            P(group, pairs, None),
            P(),
            P(),
            P(),
            P("own", blocks, None),
            P("own", blocks, None),
        ),
        check_vma=False,
    )
```

```python
import functools

import jax
import jax.numpy as jnp
from jax import lax
from jax.experimental import pallas as pl
from jax.experimental.pallas import tpu as pltpu
from jax.sharding import Mesh, PartitionSpec as P

CAP = 56
NX = 4
SLOTS = 64
PAD = 16

score_scale = 20.0
learn_rate = 0.1
norm_eps = 1e-06

bf16 = jnp.bfloat16
f32 = jnp.float32
i32 = jnp.int32


def normalize(values):
    factor = lax.rsqrt(jnp.sum(values * values, axis=-1, keepdims=True) + norm_eps)
    return (values * factor, factor)


def norm_backward(values, factor, upstream):
    inner = jnp.sum(values * upstream, axis=-1, keepdims=True)
    return factor * upstream - factor * factor * factor * values * inner


def adagrad(table, accum, grads):
    accum_new = accum + grads * grads
    return (table - learn_rate * grads * lax.rsqrt(accum_new), accum_new)


def contract_first(left, right):
    return lax.dot_general(
        left, right, (((0,), (0,)), ((), ())), preferred_element_type=f32
    )


def contract_last(left, right):
    return lax.dot_general(
        left, right, (((1,), (1,)), ((), ())), preferred_element_type=f32
    )


def exchange(blocks, axis):
    return lax.all_to_all(blocks, axis, split_axis=0, concat_axis=0, tiled=True)


def spread(block, axis):
    count = lax.axis_size(axis)
    return exchange(jnp.broadcast_to(block[None], (count,) + block.shape), axis)


def shift(block, axis, step):
    count = lax.axis_size(axis)
    return lax.ppermute(block, axis, [(i, (i + step) % count) for i in range(count)])


def reduce_blocks(blocks, axis):
    me = lax.axis_index(axis)
    got = exchange(blocks.astype(bf16), axis)
    own = lax.dynamic_index_in_dim(blocks, me, 0, keepdims=False)
    others = jnp.arange(blocks.shape[0], dtype=i32)[:, None, None] != me
    return own + jnp.sum(jnp.where(others, got.astype(f32), 0.0), axis=0)


def unpack(packed, items, log_counts):
    rows = packed[0].shape[0] - PAD
    for at, ref in enumerate(packed):
        items[pl.ds(at * rows, rows), :] = ref[:rows, :]
        tail = ref[rows:, :].astype(f32)
        logs = jnp.log(tail[:1] * 256.0 + tail[1:2])
        log_counts[pl.ds(at * rows, rows), :] = jnp.broadcast_to(logs, (128, rows)).T


def scores_of(items, log_counts, users):
    logits = score_scale * contract_last(items[...], users)
    return logits - jnp.tile(log_counts[...], (1, users.shape[0] // 128))


def sums_kernel(*refs):
    users, packed, (sums, items, log_counts) = refs[0], refs[1:-3], refs[-3:]
    unpack(packed, items, log_counts)
    tiles, tile = sums.shape[1], sums.shape[2]

    def step(t, carry):
        part = jnp.exp(scores_of(items, log_counts, users[pl.ds(t * tile, tile), :]))
        part = jnp.sum(part, axis=0, keepdims=True)
        for at in range(sums.shape[0]):
            sums[at, pl.ds(t, 1), :] = part
        return carry

    lax.fori_loop(0, tiles, step, 0)


def grads_kernel(*refs):
    place, users, sums = refs[:3]
    packed, (user_part, item_part, items, log_counts, total, lse) = refs[3:-6], refs[-6:]
    unpack(packed, items, log_counts)
    tiles, tile = sums.shape[1], sums.shape[2]
    lse[...] = jnp.log(jnp.sum(sums[...], axis=0))
    total[...] = jnp.zeros(total.shape, f32)
    shape = (items.shape[0], tile)
    apart = lax.broadcasted_iota(i32, shape, 0) - lax.broadcasted_iota(i32, shape, 1)

    def step(t, carry):
        mine = users[pl.ds(t * tile, tile), :]
        values = jnp.exp(scores_of(items, log_counts, mine) - lse[pl.ds(t, 1), :])
        wanted = jnp.where(t == place[0], 0, shape[0])
        values = jnp.where(apart == wanted, values - 1.0, values).astype(bf16)
        total[...] += jnp.dot(values, mine, preferred_element_type=f32)
        user_part[pl.ds(t * tile, tile), :] = score_scale * contract_first(values, items[...])
        return carry

    lax.fori_loop(0, tiles, step, 0)
    item_part[...] = score_scale * total[...]


def kernel_call(body, outs, scratch, flops):
    whole = pl.BlockSpec(memory_space=pltpu.VMEM)
    return functools.partial(
        pl.pallas_call,
        body,
        out_shape=outs,
        out_specs=jax.tree.map(lambda _: whole, outs),
        scratch_shapes=scratch,
        compiler_params=pltpu.CompilerParams(vmem_limit_bytes=48 << 20),
        cost_estimate=pl.CostEstimate(flops=flops, bytes_accessed=4 << 20, transcendentals=2 << 20),
    )


def on_device(
    user_vec,
    item_rows,
    w_item,
    item_count,
    item_owner,
    hot_row,
    cold_offset,
    hot_table,
    hot_accum,
    cold_table,
    cold_accum,
):
    owners = lax.axis_size("own")
    ny = lax.axis_size("ny")
    nx = lax.axis_size("nx")
    user_float = user_vec[0].astype(f32)
    item_block = item_rows[0]
    batch_rows, width = item_block.shape
    with jax.named_scope("users_along_y"):
        user_norm, user_factor = normalize(user_float)
        user_unit = user_norm.astype(bf16)
        users = spread(user_unit, "ny").reshape(ny * batch_rows, width)
    with jax.named_scope("items_along_x"):
        item_vec = jnp.dot(item_block, w_item, preferred_element_type=f32)
        item_norm, item_factor = normalize(item_vec)
        item_unit = item_norm.astype(bf16)
        counts = item_count[0]
        count_rows = jnp.stack([counts // 256, counts % 256]).astype(bf16)
        packed = jnp.concatenate(
            [item_unit, jnp.pad(count_rows, ((0, PAD - 2), (0, 0)))], axis=0
        )
        blocks = [packed] + [shift(packed, "nx", k) for k in range(1, nx)]
    pairs = (nx * batch_rows, width)
    tables = [pltpu.VMEM(pairs, bf16), pltpu.VMEM((pairs[0], 128), f32)]
    whole = pl.BlockSpec(memory_space=pltpu.VMEM)
    work = 2 * nx * ny * batch_rows * batch_rows * width
    with jax.named_scope("sums_along_y"):
        part_sums = kernel_call(
            sums_kernel, jax.ShapeDtypeStruct((ny, ny, batch_rows), f32), tables, work
        )(in_specs=[whole] * (1 + nx))(users, *blocks)
        sums = exchange(part_sums, "ny")
    with jax.named_scope("score_grad"):
        user_part, item_part = kernel_call(
            grads_kernel,
            (
                jax.ShapeDtypeStruct((ny * batch_rows, width), f32),
                jax.ShapeDtypeStruct(pairs, f32),
            ),
            tables + [pltpu.VMEM(pairs, f32), pltpu.VMEM((ny, batch_rows), f32)],
            3 * work,
        )(in_specs=[pl.BlockSpec(memory_space=pltpu.SMEM)] + [whole] * (2 + nx))(
            lax.axis_index("ny").reshape(1).astype(i32), users, sums, *blocks
        )
    with jax.named_scope("item_grad"):
        parts = item_part.reshape(nx, batch_rows, width)
        item_unit_grad = parts[0]
        for k in range(1, nx):
            item_unit_grad += shift(parts[k].astype(bf16), "nx", nx - k).astype(f32)
        item_vec_grad = norm_backward(item_vec, item_factor, item_unit_grad).astype(bf16)
        row_grad = contract_last(item_vec_grad, w_item).astype(bf16)
    with jax.named_scope("user_grad"):
        user_unit_grad = lax.psum_scatter(
            user_part.reshape(ny, batch_rows, width), "ny", scatter_dimension=0, tiled=False
        )
        user_grad = norm_backward(user_float, user_factor, user_unit_grad).astype(bf16)
    owner_id = item_owner[0, :, 0]
    with jax.named_scope("hot_and_w"):
        w_local = contract_first(item_block, item_vec_grad)
        hot_count = hot_table.shape[0]
        hot_match = (hot_row[0][:, None] == jnp.arange(hot_count, dtype=i32)[None, :]) & (
            owner_id == owners
        )[:, None]
        hot_local = contract_first(hot_match.astype(bf16), row_grad)
        half = width // 2
        rows = hot_count + width
        core = lax.axis_index("rep")
        halves = jnp.stack(
            [
                jnp.concatenate([part[:, at * half : (at + 1) * half] for part in (hot_local, w_local)])
                for at in range(2)
            ]
        )
        chip = lax.dynamic_index_in_dim(halves, core, 0, keepdims=False) + shift(
            lax.dynamic_index_in_dim(halves, 1 - core, 0, keepdims=False), "rep", 1
        )
        quarters = chip.reshape(nx, rows // nx, half)
        my_x = lax.axis_index("nx")
        line = lax.dynamic_index_in_dim(quarters, my_x, 0, keepdims=False)
        for k in range(1, nx):
            line += shift(
                lax.dynamic_index_in_dim(quarters, (my_x + k) % nx, 0, keepdims=False), "nx", k
            )
        plane = jnp.sum(exchange(line.reshape(ny, rows // (nx * ny), half), "ny"), axis=0)
        total = jnp.sum(spread(plane, "own"), axis=0)
        mine = spread(total, ("nx", "ny")).reshape(rows, half)
        other = shift(mine, "rep", 1)
        summed = jnp.concatenate(
            [jnp.where(core == 0, mine, other), jnp.where(core == 0, other, mine)], axis=1
        )
        hot_table_new, hot_accum_new = adagrad(hot_table, hot_accum, summed[:hot_count])
        w_grad = summed[hot_count:]
    with jax.named_scope("cold"):
        owner_hits = (owner_id[:, None] == jnp.arange(owners, dtype=i32)[None, :]).astype(bf16)
        place = jnp.arange(batch_rows, dtype=i32)
        earlier = (place[:, None] > place[None, :]).astype(bf16)
        before = jnp.dot(earlier, owner_hits, preferred_element_type=f32)
        slot = jnp.sum(before * owner_hits.astype(f32), axis=1).astype(i32)
        target = jnp.where(owner_id < owners, owner_id * SLOTS + slot, -1)
        placed = (
            jnp.arange(owners * SLOTS, dtype=i32)[:, None] == target[None, :]
        ).astype(bf16)
        mark = cold_offset[0] + 1
        slot_hits = (slot[:, None] == jnp.arange(SLOTS, dtype=i32)[None, :]).astype(bf16)
        high = contract_first(owner_hits * (mark // 256).astype(bf16)[:, None], slot_hits)
        low = contract_first(owner_hits * (mark % 256).astype(bf16)[:, None], slot_hits)
        marks = jnp.concatenate([high, low], axis=1).astype(bf16)
        marks = jnp.pad(marks[:, None, :], ((0, 0), (0, SLOTS - CAP - 1), (0, width - 2 * SLOTS)))
        send_rows = jnp.dot(placed, row_grad, preferred_element_type=f32).astype(bf16)
        send_rows = send_rows.reshape(owners, SLOTS, width)[:, :CAP]
        got = exchange(jnp.concatenate([send_rows, marks], axis=1), "own")
        got_marks = got[:, CAP].astype(f32)
        offsets = (got_marks[:, :SLOTS] * 256.0 + got_marks[:, SLOTS : 2 * SLOTS]).astype(i32) - 1
        local_rows = cold_table.shape[1]
        lands = (
            jnp.arange(local_rows, dtype=i32)[:, None] == offsets.reshape(-1)[None, :]
        ).astype(bf16)
        cold_grad = jnp.dot(
            lands, got.reshape(owners * SLOTS, width), preferred_element_type=f32
        )
        cold_table_new, cold_accum_new = adagrad(cold_table[0], cold_accum[0], cold_grad)
    return (
        user_grad[None],
        w_grad,
        hot_table_new,
        hot_accum_new,
        cold_table_new[None],
        cold_accum_new[None],
    )


def solution(mesh):
    owners, neg, rep = (mesh.shape[name] for name in ("own", "neg", "rep"))
    grid = Mesh(
        mesh.devices.reshape(owners, NX, neg // NX, rep), ("own", "nx", "ny", "rep")
    )
    group, pairs, blocks = ("own", "rep"), ("nx", "ny"), ("nx", "ny", "rep")
    return jax.shard_map(
        on_device,
        mesh=grid,
        in_specs=(
            P(group, pairs, None),
            P(group, pairs, None),
            P(),
            P(group, pairs),
            P(group, pairs, None),
            P(group, pairs),
            P(group, pairs),
            P(),
            P(),
            P("own", blocks, None),
            P("own", blocks, None),
        ),
        out_specs=(
            P(group, pairs, None),
            P(),
            P(),
            P(),
            P("own", blocks, None),
            P("own", blocks, None),
        ),
        check_vma=False,
    )
```

```python
import functools

import jax
import jax.numpy as jnp
from jax import lax
from jax.experimental import pallas as pl
from jax.experimental.pallas import tpu as pltpu
from jax.sharding import Mesh, PartitionSpec as P

CAP = 56
NX = 4
SLOTS = 64
PAD = 16

score_scale = 20.0
learn_rate = 0.1
norm_eps = 1e-06

bf16 = jnp.bfloat16
f32 = jnp.float32
i32 = jnp.int32


def normalize(values):
    factor = lax.rsqrt(jnp.sum(values * values, axis=-1, keepdims=True) + norm_eps)
    return (values * factor, factor)


def norm_backward(values, factor, upstream):
    inner = jnp.sum(values * upstream, axis=-1, keepdims=True)
    return factor * upstream - factor * factor * factor * values * inner


def adagrad(table, accum, grads):
    accum_new = accum + grads * grads
    return (table - learn_rate * grads * lax.rsqrt(accum_new), accum_new)


def contract_first(left, right):
    return lax.dot_general(
        left, right, (((0,), (0,)), ((), ())), preferred_element_type=f32
    )


def contract_last(left, right):
    return lax.dot_general(
        left, right, (((1,), (1,)), ((), ())), preferred_element_type=f32
    )


def exchange(blocks, axis):
    return lax.all_to_all(blocks, axis, split_axis=0, concat_axis=0, tiled=True)


def spread(block, axis):
    count = lax.axis_size(axis)
    return exchange(jnp.broadcast_to(block[None], (count,) + block.shape), axis)


def shift(block, axis, step):
    count = lax.axis_size(axis)
    return lax.ppermute(block, axis, [(i, (i + step) % count) for i in range(count)])


def unpack(packed, items, log_counts):
    rows = packed[0].shape[0] - PAD
    for at, ref in enumerate(packed):
        items[pl.ds(at * rows, rows), :] = ref[:rows, :]
        tail = ref[rows:, :].astype(f32)
        logs = jnp.log(tail[:1] * 256.0 + tail[1:2])
        log_counts[pl.ds(at * rows, rows), :] = jnp.broadcast_to(logs, (128, rows)).T


def sums_kernel(*refs):
    users, packed, (sums, weights, items, log_counts) = refs[0], refs[1:-4], refs[-4:]
    unpack(packed, items, log_counts)
    tiles, tile = sums.shape[1], sums.shape[2]
    logs = jnp.tile(log_counts[...], (1, tile // 128))
    for t in range(tiles):
        mine = slice(t * tile, (t + 1) * tile)
        values = jnp.exp(score_scale * contract_last(items[...], users[mine, :]) - logs)
        weights[:, mine] = values
        part = jnp.sum(values, axis=0, keepdims=True)
        for at in range(sums.shape[0]):
            sums[at, t : t + 1, :] = part


def grads_kernel(place, users, sums, weights, score_grad, item_send, item_own):
    tiles, tile = sums.shape[1], sums.shape[2]
    inverse = 1.0 / jnp.sum(sums[...], axis=0)
    square = (tile, tile)
    eye = lax.broadcasted_iota(i32, square, 0) == lax.broadcasted_iota(i32, square, 1)
    for t in range(tiles):
        mine = slice(t * tile, (t + 1) * tile)
        score_grad[:, mine] = (weights[:, mine] * inverse[t : t + 1, :]).astype(bf16)

        @pl.when(place[1] == t)
        def _():
            values = weights[:tile, mine] * inverse[t : t + 1, :]
            score_grad[:tile, mine] = jnp.where(eye, values - 1.0, values).astype(bf16)

    total = score_scale * jnp.dot(score_grad[...], users[...], preferred_element_type=f32)
    count, rows = item_send.shape[0], item_send.shape[1]
    item_own[...] = total[:rows]
    for k in range(count):
        item_send[lax.rem(place[0] + (count - k), count)] = total[
            k * rows : (k + 1) * rows
        ].astype(bf16)


def kernel_call(body, outs, scratch, flops):
    whole = pl.BlockSpec(memory_space=pltpu.VMEM)
    return functools.partial(
        pl.pallas_call,
        body,
        out_shape=outs,
        out_specs=jax.tree.map(lambda _: whole, outs),
        scratch_shapes=scratch,
        compiler_params=pltpu.CompilerParams(vmem_limit_bytes=24 << 20),
        cost_estimate=pl.CostEstimate(flops=flops, bytes_accessed=4 << 20, transcendentals=2 << 20),
    )


def on_device(
    user_vec,
    item_rows,
    w_item,
    item_count,
    item_owner,
    hot_row,
    cold_offset,
    hot_table,
    hot_accum,
    cold_table,
    cold_accum,
):
    owners = lax.axis_size("own")
    ny = lax.axis_size("ny")
    nx = lax.axis_size("nx")
    user_float = user_vec[0].astype(f32)
    item_block = item_rows[0]
    batch_rows, width = item_block.shape
    with jax.named_scope("users_along_y"):
        user_norm, user_factor = normalize(user_float)
        user_unit = user_norm.astype(bf16)
        users = spread(user_unit, "ny").reshape(ny * batch_rows, width)
    with jax.named_scope("items_along_x"):
        item_vec = jnp.dot(item_block, w_item, preferred_element_type=f32)
        item_norm, item_factor = normalize(item_vec)
        item_unit = item_norm.astype(bf16)
        counts = item_count[0]
        count_rows = jnp.stack([counts // 256, counts % 256]).astype(bf16)
        packed = jnp.concatenate(
            [item_unit, jnp.pad(count_rows, ((0, PAD - 2), (0, 0)))], axis=0
        )
        blocks = [packed] + [shift(packed, "nx", k) for k in range(1, nx)]
    pairs = (nx * batch_rows, width)
    grid = (nx * batch_rows, ny * batch_rows)
    whole = pl.BlockSpec(memory_space=pltpu.VMEM)
    work = 2 * nx * ny * batch_rows * batch_rows * width
    my_x, my_y = lax.axis_index("nx"), lax.axis_index("ny")
    with jax.named_scope("sums_along_y"):
        part_sums, weights, items = kernel_call(
            sums_kernel,
            (
                jax.ShapeDtypeStruct((ny, ny, batch_rows), f32),
                jax.ShapeDtypeStruct(grid, f32),
                jax.ShapeDtypeStruct(pairs, bf16),
            ),
            [pltpu.VMEM((pairs[0], 128), f32)],
            work,
        )(in_specs=[whole] * (1 + nx))(users, *blocks)
        sums = exchange(part_sums, "ny")
    with jax.named_scope("score_grad"):
        score_grad, item_send, item_own = kernel_call(
            grads_kernel,
            (
                jax.ShapeDtypeStruct(grid, bf16),
                jax.ShapeDtypeStruct((nx, batch_rows, width), bf16),
                jax.ShapeDtypeStruct((batch_rows, width), f32),
            ),
            [],
            work,
        )(in_specs=[pl.BlockSpec(memory_space=pltpu.SMEM)] + [whole] * 3)(
            jnp.stack([my_x, my_y]).astype(i32), users, sums, weights
        )
    with jax.named_scope("item_grad"):
        item_got = exchange(item_send, "nx").astype(f32)
        others = jnp.arange(nx, dtype=i32)[:, None, None] != my_x
        item_unit_grad = item_own + jnp.sum(jnp.where(others, item_got, 0.0), axis=0)
        item_vec_grad = norm_backward(item_vec, item_factor, item_unit_grad).astype(bf16)
        row_grad = contract_last(item_vec_grad, w_item).astype(bf16)
    with jax.named_scope("user_grad"):
        user_part = score_scale * contract_first(score_grad, items)
        user_unit_grad = lax.psum_scatter(
            user_part.reshape(ny, batch_rows, width), "ny", scatter_dimension=0, tiled=False
        )
        user_grad = norm_backward(user_float, user_factor, user_unit_grad).astype(bf16)
    owner_id = item_owner[0, :, 0]
    with jax.named_scope("hot_and_w"):
        w_local = contract_first(item_block, item_vec_grad)
        hot_count = hot_table.shape[0]
        hot_match = (hot_row[0][:, None] == jnp.arange(hot_count, dtype=i32)[None, :]) & (
            owner_id == owners
        )[:, None]
        hot_local = contract_first(hot_match.astype(bf16), row_grad)
        half = width // 2
        rows = hot_count + width
        core = lax.axis_index("rep")
        halves = jnp.stack(
            [
                jnp.concatenate([part[:, at * half : (at + 1) * half] for part in (hot_local, w_local)])
                for at in range(2)
            ]
        )
        chip = lax.dynamic_index_in_dim(halves, core, 0, keepdims=False) + shift(
            lax.dynamic_index_in_dim(halves, 1 - core, 0, keepdims=False), "rep", 1
        )
        plane = jnp.sum(
            exchange(chip.reshape(nx * ny, rows // (nx * ny), half), ("nx", "ny")), axis=0
        )
        plane_high = plane.astype(bf16)
        plane_low = (plane - plane_high.astype(f32)).astype(bf16)
        plane_rows = jnp.concatenate([plane_high, plane_low], axis=1)
    with jax.named_scope("cold"):
        owner_hits = (owner_id[:, None] == jnp.arange(owners, dtype=i32)[None, :]).astype(bf16)
        place = jnp.arange(batch_rows, dtype=i32)
        earlier = (place[:, None] > place[None, :]).astype(bf16)
        before = jnp.dot(earlier, owner_hits, preferred_element_type=f32)
        slot = jnp.sum(before * owner_hits.astype(f32), axis=1).astype(i32)
        target = jnp.where(owner_id < owners, owner_id * SLOTS + slot, -1)
        placed = (
            jnp.arange(owners * SLOTS, dtype=i32)[:, None] == target[None, :]
        ).astype(bf16)
        mark = cold_offset[0] + 1
        slot_hits = (slot[:, None] == jnp.arange(SLOTS, dtype=i32)[None, :]).astype(bf16)
        high = contract_first(owner_hits * (mark // 256).astype(bf16)[:, None], slot_hits)
        low = contract_first(owner_hits * (mark % 256).astype(bf16)[:, None], slot_hits)
        marks = jnp.concatenate([high, low], axis=1).astype(bf16)
        marks = jnp.pad(marks[:, None, :], ((0, 0), (0, SLOTS - CAP - 1), (0, width - 2 * SLOTS)))
        send_rows = jnp.dot(placed, row_grad, preferred_element_type=f32).astype(bf16)
        send_rows = send_rows.reshape(owners, SLOTS, width)[:, :CAP]
        to_all = jnp.broadcast_to(plane_rows[None], (owners,) + plane_rows.shape)
        got = exchange(jnp.concatenate([send_rows, marks, to_all], axis=1), "own")
        got_marks = got[:, CAP].astype(f32)
        offsets = (got_marks[:, :SLOTS] * 256.0 + got_marks[:, SLOTS : 2 * SLOTS]).astype(i32) - 1
        local_rows = cold_table.shape[1]
        lands = (
            jnp.arange(local_rows, dtype=i32)[:, None] == offsets.reshape(-1)[None, :]
        ).astype(bf16)
        cold_grad = jnp.dot(
            lands, got[:, :SLOTS].reshape(owners * SLOTS, width), preferred_element_type=f32
        )
        cold_table_new, cold_accum_new = adagrad(cold_table[0], cold_accum[0], cold_grad)
    with jax.named_scope("hot_and_w_back"):
        got_plane = got[:, SLOTS:].astype(f32)
        total = jnp.sum(got_plane[:, :, :half] + got_plane[:, :, half:], axis=0)
        mine = spread(total, ("nx", "ny")).reshape(rows, half)
        mine, user_grad, cold_table_new, cold_accum_new = lax.optimization_barrier(
            (mine, user_grad, cold_table_new, cold_accum_new)
        )
        other = shift(mine, "rep", 1)
        summed = jnp.concatenate(
            [jnp.where(core == 0, mine, other), jnp.where(core == 0, other, mine)], axis=1
        )
        hot_table_new, hot_accum_new = adagrad(hot_table, hot_accum, summed[:hot_count])
        w_grad = summed[hot_count:]
    return (
        user_grad[None],
        w_grad,
        hot_table_new,
        hot_accum_new,
        cold_table_new[None],
        cold_accum_new[None],
    )


def solution(mesh):
    owners, neg, rep = (mesh.shape[name] for name in ("own", "neg", "rep"))
    grid = Mesh(
        mesh.devices.reshape(owners, NX, neg // NX, rep), ("own", "nx", "ny", "rep")
    )
    group, pairs, blocks = ("own", "rep"), ("nx", "ny"), ("nx", "ny", "rep")
    return jax.shard_map(
        on_device,
        mesh=grid,
        in_specs=(
            P(group, pairs, None),
            P(group, pairs, None),
            P(),
            P(group, pairs),
            P(group, pairs, None),
            P(group, pairs),
            P(group, pairs),
            P(),
            P(),
            P("own", blocks, None),
            P("own", blocks, None),
        ),
        out_specs=(
            P(group, pairs, None),
            P(),
            P(),
            P(),
            P("own", blocks, None),
            P("own", blocks, None),
        ),
        check_vma=False,
    )
```

```python
import functools

import jax
import jax.numpy as jnp
from jax import lax
from jax.experimental import pallas as pl
from jax.experimental.pallas import tpu as pltpu
from jax.sharding import Mesh, PartitionSpec as P

CAP = 56
NX = 4
SLOTS = 64
PAD = 16

score_scale = 20.0
learn_rate = 0.1
norm_eps = 1e-06

bf16 = jnp.bfloat16
f32 = jnp.float32
i32 = jnp.int32


def normalize(values):
    factor = lax.rsqrt(jnp.sum(values * values, axis=-1, keepdims=True) + norm_eps)
    return (values * factor, factor)


def norm_backward(values, factor, upstream):
    inner = jnp.sum(values * upstream, axis=-1, keepdims=True)
    return factor * upstream - factor * factor * factor * values * inner


def adagrad(table, accum, grads):
    accum_new = accum + grads * grads
    return (table - learn_rate * grads * lax.rsqrt(accum_new), accum_new)


def contract_first(left, right):
    return lax.dot_general(
        left, right, (((0,), (0,)), ((), ())), preferred_element_type=f32
    )


def contract_last(left, right):
    return lax.dot_general(
        left, right, (((1,), (1,)), ((), ())), preferred_element_type=f32
    )


def exchange(blocks, axis):
    return lax.all_to_all(blocks, axis, split_axis=0, concat_axis=0, tiled=True)


def spread(block, axis):
    count = lax.axis_size(axis)
    return exchange(jnp.broadcast_to(block[None], (count,) + block.shape), axis)


def shift(block, axis, step):
    count = lax.axis_size(axis)
    return lax.ppermute(block, axis, [(i, (i + step) % count) for i in range(count)])


def unpack(packed, items, log_counts):
    rows = packed[0].shape[0] - PAD
    for at, ref in enumerate(packed):
        items[pl.ds(at * rows, rows), :] = ref[:rows, :]
        tail = ref[rows:, :].astype(f32)
        logs = jnp.log(tail[:1] * 256.0 + tail[1:2])
        log_counts[pl.ds(at * rows, rows), :] = jnp.broadcast_to(logs, (128, rows)).T


def scores_of(items, log_counts, users):
    logs = jnp.tile(log_counts[...], (1, users.shape[0] // 128))
    return jnp.exp(score_scale * contract_last(items[...], users) - logs)


def sums_kernel(*refs):
    users, packed, (sums, items, log_counts) = refs[0], refs[1:-3], refs[-3:]
    unpack(packed, items, log_counts)
    tiles, tile = sums.shape[1], sums.shape[2]
    for t in range(tiles):
        values = scores_of(items, log_counts, users[t * tile : (t + 1) * tile, :])
        part = jnp.sum(values, axis=0, keepdims=True)
        for at in range(sums.shape[0]):
            sums[at, t : t + 1, :] = part


def grads_kernel(
    place, users, sums, items, log_counts, user_send, user_own, item_send, item_own, score_grad
):
    tiles, tile = sums.shape[1], sums.shape[2]
    inverse = 1.0 / jnp.sum(sums[...], axis=0)
    square = (tile, tile)
    eye = lax.broadcasted_iota(i32, square, 0) == lax.broadcasted_iota(i32, square, 1)
    for t in range(tiles):
        mine = slice(t * tile, (t + 1) * tile)
        values = scores_of(items, log_counts, users[mine, :]) * inverse[t : t + 1, :]
        own = jnp.where(eye & (place[1] == t), values[:tile] - 1.0, values[:tile])
        score_grad[:tile, mine] = own.astype(bf16)
        score_grad[tile:, mine] = values[tile:].astype(bf16)
        part = score_scale * contract_first(score_grad[:, mine], items[...])
        user_send[lax.rem(t + tiles - place[1], tiles)] = part.astype(bf16)

        @pl.when(place[1] == t)
        def _():
            user_own[...] = part

    total = score_scale * jnp.dot(score_grad[...], users[...], preferred_element_type=f32)
    count, rows = item_send.shape[0], item_send.shape[1]
    item_own[...] = total[:rows]
    for k in range(count):
        item_send[lax.rem(place[0] + (count - k), count)] = total[
            k * rows : (k + 1) * rows
        ].astype(bf16)


def kernel_call(body, outs, scratch, flops):
    whole = pl.BlockSpec(memory_space=pltpu.VMEM)
    return functools.partial(
        pl.pallas_call,
        body,
        out_shape=outs,
        out_specs=jax.tree.map(lambda _: whole, outs),
        scratch_shapes=scratch,
        compiler_params=pltpu.CompilerParams(vmem_limit_bytes=24 << 20),
        cost_estimate=pl.CostEstimate(flops=flops, bytes_accessed=4 << 20, transcendentals=2 << 20),
    )


def on_device(
    user_vec,
    item_rows,
    w_item,
    item_count,
    item_owner,
    hot_row,
    cold_offset,
    hot_table,
    hot_accum,
    cold_table,
    cold_accum,
):
    owners = lax.axis_size("own")
    ny = lax.axis_size("ny")
    nx = lax.axis_size("nx")
    user_float = user_vec[0].astype(f32)
    item_block = item_rows[0]
    batch_rows, width = item_block.shape
    with jax.named_scope("users_along_y"):
        user_norm, user_factor = normalize(user_float)
        user_unit = user_norm.astype(bf16)
        users = spread(user_unit, "ny").reshape(ny * batch_rows, width)
    with jax.named_scope("items_along_x"):
        item_vec = jnp.dot(item_block, w_item, preferred_element_type=f32)
        item_norm, item_factor = normalize(item_vec)
        item_unit = item_norm.astype(bf16)
        counts = item_count[0]
        count_rows = jnp.stack([counts // 256, counts % 256]).astype(bf16)
        packed = jnp.concatenate(
            [item_unit, jnp.pad(count_rows, ((0, PAD - 2), (0, 0)))], axis=0
        )
        blocks = [packed] + [shift(packed, "nx", k) for k in range(1, nx)]
    pairs = (nx * batch_rows, width)
    whole = pl.BlockSpec(memory_space=pltpu.VMEM)
    work = 2 * nx * ny * batch_rows * batch_rows * width
    my_x, my_y = lax.axis_index("nx"), lax.axis_index("ny")
    with jax.named_scope("sums_along_y"):
        part_sums, items, log_counts = kernel_call(
            sums_kernel,
            (
                jax.ShapeDtypeStruct((ny, ny, batch_rows), f32),
                jax.ShapeDtypeStruct(pairs, bf16),
                jax.ShapeDtypeStruct((pairs[0], 128), f32),
            ),
            [],
            work,
        )(in_specs=[whole] * (1 + nx))(users, *blocks)
        sums = exchange(part_sums, "ny")
    with jax.named_scope("score_grad"):
        user_send, user_own, item_send, item_own = kernel_call(
            grads_kernel,
            (
                jax.ShapeDtypeStruct((ny, batch_rows, width), bf16),
                jax.ShapeDtypeStruct((batch_rows, width), f32),
                jax.ShapeDtypeStruct((nx, batch_rows, width), bf16),
                jax.ShapeDtypeStruct((batch_rows, width), f32),
            ),
            [pltpu.VMEM((pairs[0], ny * batch_rows), bf16)],
            3 * work,
        )(in_specs=[pl.BlockSpec(memory_space=pltpu.SMEM)] + [whole] * 4)(
            jnp.stack([my_x, my_y]).astype(i32), users, sums, items, log_counts
        )
    with jax.named_scope("item_grad"):
        item_got = exchange(item_send, "nx").astype(f32)
        others = jnp.arange(nx, dtype=i32)[:, None, None] != my_x
        item_unit_grad = item_own + jnp.sum(jnp.where(others, item_got, 0.0), axis=0)
        item_vec_grad = norm_backward(item_vec, item_factor, item_unit_grad).astype(bf16)
        row_grad = contract_last(item_vec_grad, w_item).astype(bf16)
    owner_id = item_owner[0, :, 0]
    with jax.named_scope("hot_and_w"):
        w_local = contract_first(item_block, item_vec_grad)
        hot_count = hot_table.shape[0]
        hot_match = (hot_row[0][:, None] == jnp.arange(hot_count, dtype=i32)[None, :]) & (
            owner_id == owners
        )[:, None]
        hot_local = contract_first(hot_match.astype(bf16), row_grad)
        half = width // 2
        rows = hot_count + width
        core = lax.axis_index("rep")
        halves = jnp.stack(
            [
                jnp.concatenate([part[:, at * half : (at + 1) * half] for part in (hot_local, w_local)])
                for at in range(2)
            ]
        )
        chip = lax.dynamic_index_in_dim(halves, core, 0, keepdims=False) + shift(
            lax.dynamic_index_in_dim(halves, 1 - core, 0, keepdims=False), "rep", 1
        )
        late = range(ny // 4 + 1, ny - ny // 4 + 1)
        chip, user_soon = lax.optimization_barrier((chip, user_send))
        user_got = {k: shift(user_soon[k], "ny", k) for k in range(1, ny) if k not in late}
        plane = jnp.sum(
            exchange(chip.reshape(nx * ny, rows // (nx * ny), half), ("nx", "ny")), axis=0
        )
        plane_high = lax.reduce_precision(plane, exponent_bits=8, mantissa_bits=7)
        plane_rows = jnp.concatenate([plane_high, plane - plane_high], axis=1).astype(bf16)
        plane_rows, user_late, user_got = lax.optimization_barrier(
            (plane_rows, user_soon, user_got)
        )
    with jax.named_scope("user_grad"):
        user_unit_grad = user_own
        for k in range(1, ny):
            got_part = shift(user_late[k], "ny", k) if k in late else user_got[k]
            user_unit_grad += got_part.astype(f32)
        user_grad = norm_backward(user_float, user_factor, user_unit_grad).astype(bf16)
    with jax.named_scope("cold"):
        owner_hits = (owner_id[:, None] == jnp.arange(owners, dtype=i32)[None, :]).astype(bf16)
        place = jnp.arange(batch_rows, dtype=i32)
        earlier = (place[:, None] > place[None, :]).astype(bf16)
        before = jnp.dot(earlier, owner_hits, preferred_element_type=f32)
        slot = jnp.sum(before * owner_hits.astype(f32), axis=1).astype(i32)
        target = jnp.where(owner_id < owners, owner_id * SLOTS + slot, -1)
        placed = (
            jnp.arange(owners * SLOTS, dtype=i32)[:, None] == target[None, :]
        ).astype(bf16)
        mark = cold_offset[0] + 1
        slot_hits = (slot[:, None] == jnp.arange(SLOTS, dtype=i32)[None, :]).astype(bf16)
        high = contract_first(owner_hits * (mark // 256).astype(bf16)[:, None], slot_hits)
        low = contract_first(owner_hits * (mark % 256).astype(bf16)[:, None], slot_hits)
        marks = jnp.concatenate([high, low], axis=1).astype(bf16)
        marks = jnp.pad(marks[:, None, :], ((0, 0), (0, SLOTS - CAP - 1), (0, width - 2 * SLOTS)))
        send_rows = jnp.dot(placed, row_grad, preferred_element_type=f32).astype(bf16)
        send_rows = send_rows.reshape(owners, SLOTS, width)[:, :CAP]
        to_all = jnp.broadcast_to(plane_rows[None], (owners,) + plane_rows.shape)
        got = exchange(jnp.concatenate([send_rows, marks, to_all], axis=1), "own")
        got_marks = got[:, CAP].astype(f32)
        offsets = (got_marks[:, :SLOTS] * 256.0 + got_marks[:, SLOTS : 2 * SLOTS]).astype(i32) - 1
        local_rows = cold_table.shape[1]
        lands = (
            jnp.arange(local_rows, dtype=i32)[:, None] == offsets.reshape(-1)[None, :]
        ).astype(bf16)
        cold_grad = jnp.dot(
            lands, got[:, :SLOTS].reshape(owners * SLOTS, width), preferred_element_type=f32
        )
        cold_table_new, cold_accum_new = adagrad(cold_table[0], cold_accum[0], cold_grad)
    with jax.named_scope("hot_and_w_back"):
        got_plane = got[:, SLOTS:].astype(f32)
        total = jnp.sum(got_plane[:, :, :half] + got_plane[:, :, half:], axis=0)
        mine = spread(total, ("nx", "ny")).reshape(rows, half)
        mine, user_grad, cold_table_new, cold_accum_new = lax.optimization_barrier(
            (mine, user_grad, cold_table_new, cold_accum_new)
        )
        other = shift(mine, "rep", 1)
        summed = jnp.concatenate(
            [jnp.where(core == 0, mine, other), jnp.where(core == 0, other, mine)], axis=1
        )
        hot_table_new, hot_accum_new = adagrad(hot_table, hot_accum, summed[:hot_count])
        w_grad = summed[hot_count:]
    return (
        user_grad[None],
        w_grad,
        hot_table_new,
        hot_accum_new,
        cold_table_new[None],
        cold_accum_new[None],
    )


def solution(mesh):
    owners, neg, rep = (mesh.shape[name] for name in ("own", "neg", "rep"))
    grid = Mesh(
        mesh.devices.reshape(owners, NX, neg // NX, rep), ("own", "nx", "ny", "rep")
    )
    group, pairs, blocks = ("own", "rep"), ("nx", "ny"), ("nx", "ny", "rep")
    return jax.shard_map(
        on_device,
        mesh=grid,
        in_specs=(
            P(group, pairs, None),
            P(group, pairs, None),
            P(),
            P(group, pairs),
            P(group, pairs, None),
            P(group, pairs),
            P(group, pairs),
            P(),
            P(),
            P("own", blocks, None),
            P("own", blocks, None),
        ),
        out_specs=(
            P(group, pairs, None),
            P(),
            P(),
            P(),
            P("own", blocks, None),
            P("own", blocks, None),
        ),
        check_vma=False,
    )
```

```python
import functools

import jax
import jax.numpy as jnp
from jax import lax
from jax.experimental import pallas as pl
from jax.experimental.pallas import tpu as pltpu
from jax.sharding import Mesh, PartitionSpec as P

CAP = 56
NX = 4
SLOTS = 64
PAD = 16

score_scale = 20.0
learn_rate = 0.1
norm_eps = 1e-06

bf16 = jnp.bfloat16
f32 = jnp.float32
i32 = jnp.int32


def normalize(values):
    factor = lax.rsqrt(jnp.sum(values * values, axis=-1, keepdims=True) + norm_eps)
    return (values * factor, factor)


def norm_backward(values, factor, upstream):
    inner = jnp.sum(values * upstream, axis=-1, keepdims=True)
    return factor * upstream - factor * factor * factor * values * inner


def adagrad(table, accum, grads):
    accum_new = accum + grads * grads
    return (table - learn_rate * grads * lax.rsqrt(accum_new), accum_new)


def contract_first(left, right):
    return lax.dot_general(
        left, right, (((0,), (0,)), ((), ())), preferred_element_type=f32
    )


def contract_last(left, right):
    return lax.dot_general(
        left, right, (((1,), (1,)), ((), ())), preferred_element_type=f32
    )


def exchange(blocks, axis):
    return lax.all_to_all(blocks, axis, split_axis=0, concat_axis=0, tiled=True)


def spread(block, axis):
    count = lax.axis_size(axis)
    return exchange(jnp.broadcast_to(block[None], (count,) + block.shape), axis)


def shift(block, axis, step):
    count = lax.axis_size(axis)
    return lax.ppermute(block, axis, [(i, (i + step) % count) for i in range(count)])


def flip(block, axis, mask):
    count = lax.axis_size(axis)
    return lax.ppermute(block, axis, [(i, i ^ mask) for i in range(count)])


def unpack(packed, items, log_counts):
    rows = packed[0].shape[0] - PAD
    for at, ref in enumerate(packed):
        items[pl.ds(at * rows, rows), :] = ref[:rows, :]
        tail = ref[rows:, :].astype(f32)
        logs = jnp.log(tail[:1] * 256.0 + tail[1:2])
        log_counts[pl.ds(at * rows, rows), :] = jnp.broadcast_to(logs, (128, rows)).T


def scores_of(items, log_counts, users):
    logs = jnp.tile(log_counts[...], (1, users.shape[0] // 128))
    return jnp.exp(score_scale * contract_last(items[...], users) - logs)


def sums_kernel(*refs):
    users, packed, (sums, items, log_counts) = refs[0], refs[1:-3], refs[-3:]
    unpack(packed, items, log_counts)
    tiles, tile = sums.shape[1], sums.shape[2]
    for t in range(tiles):
        values = scores_of(items, log_counts, users[t * tile : (t + 1) * tile, :])
        part = jnp.sum(values, axis=0, keepdims=True)
        for at in range(sums.shape[0]):
            sums[at, t : t + 1, :] = part


def grads_kernel(
    place, users, sums, items, log_counts, score_grad, item_send, item_own, total
):
    t = pl.program_id(0)
    tile = users.shape[0]
    square = (tile, tile)
    eye = lax.broadcasted_iota(i32, square, 0) == lax.broadcasted_iota(i32, square, 1)
    inverse = 1.0 / jnp.sum(sums[:, pl.ds(t, 1), :], axis=0)
    values = scores_of(items, log_counts, users[...]) * inverse
    own = jnp.where(eye & (place[1] == t), values[:tile] - 1.0, values[:tile])
    score_grad[:tile, :] = own.astype(bf16)
    score_grad[tile:, :] = values[tile:].astype(bf16)
    part = jnp.dot(score_grad[...], users[...], preferred_element_type=f32)

    @pl.when(t == 0)
    def _():
        total[...] = part

    @pl.when(t > 0)
    def _():
        total[...] += part

    @pl.when(t == pl.num_programs(0) - 1)
    def _():
        count, rows = item_send.shape[0], item_send.shape[1]
        item_own[...] = score_scale * total[:rows, :]
        for k in range(count):
            item_send[lax.rem(place[0] + (count - k), count)] = (
                score_scale * total[k * rows : (k + 1) * rows, :]
            ).astype(bf16)


def users_kernel(place, even, odd, items, keep, send):
    keep[0] = score_scale * contract_first(even[...], items[...])
    send[0] = (score_scale * contract_first(odd[...], items[...])).astype(bf16)


def kernel_call(body, outs, scratch, flops):
    whole = pl.BlockSpec(memory_space=pltpu.VMEM)
    return functools.partial(
        pl.pallas_call,
        body,
        out_shape=outs,
        out_specs=jax.tree.map(lambda _: whole, outs),
        scratch_shapes=scratch,
        compiler_params=pltpu.CompilerParams(vmem_limit_bytes=24 << 20),
        cost_estimate=pl.CostEstimate(flops=flops, bytes_accessed=4 << 20, transcendentals=2 << 20),
    )


def on_device(
    user_vec,
    item_rows,
    w_item,
    item_count,
    item_owner,
    hot_row,
    cold_offset,
    hot_table,
    hot_accum,
    cold_table,
    cold_accum,
):
    owners = lax.axis_size("own")
    ny = lax.axis_size("ny")
    nx = lax.axis_size("nx")
    user_float = user_vec[0].astype(f32)
    item_block = item_rows[0]
    batch_rows, width = item_block.shape
    with jax.named_scope("users_along_y"):
        user_norm, user_factor = normalize(user_float)
        user_unit = user_norm.astype(bf16)
        users = spread(user_unit, "ny").reshape(ny * batch_rows, width)
    with jax.named_scope("items_along_x"):
        item_vec = jnp.dot(item_block, w_item, preferred_element_type=f32)
        item_norm, item_factor = normalize(item_vec)
        item_unit = item_norm.astype(bf16)
        counts = item_count[0]
        count_rows = jnp.stack([counts // 256, counts % 256]).astype(bf16)
        packed = jnp.concatenate(
            [item_unit, jnp.pad(count_rows, ((0, PAD - 2), (0, 0)))], axis=0
        )
        blocks = [packed] + [shift(packed, "nx", k) for k in range(1, nx)]
    pairs = (nx * batch_rows, width)
    whole = pl.BlockSpec(memory_space=pltpu.VMEM)
    work = 2 * nx * ny * batch_rows * batch_rows * width
    my_x, my_y = lax.axis_index("nx"), lax.axis_index("ny")
    with jax.named_scope("sums_along_y"):
        part_sums, items, log_counts = kernel_call(
            sums_kernel,
            (
                jax.ShapeDtypeStruct((ny, ny, batch_rows), f32),
                jax.ShapeDtypeStruct(pairs, bf16),
                jax.ShapeDtypeStruct((pairs[0], 128), f32),
            ),
            [],
            work,
        )(in_specs=[whole] * (1 + nx))(users, *blocks)
        sums = exchange(part_sums, "ny")
    with jax.named_scope("score_grad"):
        place = jnp.stack([my_x, my_y]).astype(i32)
        fixed = lambda shape: pl.BlockSpec(shape, lambda t, place: (0,) * len(shape))
        sent = (nx, batch_rows, width)
        score_grad, item_send, item_own = pl.pallas_call(
            grads_kernel,
            out_shape=(
                pltpu.HBM((pairs[0], ny * batch_rows), bf16),
                jax.ShapeDtypeStruct(sent, bf16),
                jax.ShapeDtypeStruct((batch_rows, width), f32),
            ),
            grid_spec=pltpu.PrefetchScalarGridSpec(
                num_scalar_prefetch=1,
                grid=(ny,),
                in_specs=[
                    pl.BlockSpec((batch_rows, width), lambda t, place: (t, 0)),
                    fixed(sums.shape),
                    fixed(pairs),
                    fixed((pairs[0], 128)),
                ],
                out_specs=(
                    pl.BlockSpec((pairs[0], batch_rows), lambda t, place: (0, t)),
                    fixed(sent),
                    fixed((batch_rows, width)),
                ),
                scratch_shapes=[pltpu.VMEM(pairs, f32)],
            ),
            compiler_params=pltpu.CompilerParams(vmem_limit_bytes=24 << 20),
            cost_estimate=pl.CostEstimate(
                flops=2 * work, bytes_accessed=8 << 20, transcendentals=2 << 20
            ),
        )(place, users, sums, items, log_counts)
    with jax.named_scope("user_part"):
        user_keep, user_send = pl.pallas_call(
            users_kernel,
            out_shape=(
                jax.ShapeDtypeStruct((ny // 2, batch_rows, width), f32),
                jax.ShapeDtypeStruct((ny // 2, batch_rows, width), bf16),
            ),
            grid_spec=pltpu.PrefetchScalarGridSpec(
                num_scalar_prefetch=1,
                grid=(ny // 2,),
                in_specs=[
                    pl.BlockSpec(
                        (pairs[0], batch_rows),
                        lambda q, place: (0, lax.bitwise_xor(2 * q, place[1])),
                    ),
                    pl.BlockSpec(
                        (pairs[0], batch_rows),
                        lambda q, place: (0, lax.bitwise_xor(2 * q + 1, place[1])),
                    ),
                    fixed(pairs),
                ],
                out_specs=(
                    pl.BlockSpec((1, batch_rows, width), lambda q, place: (q, 0, 0)),
                    pl.BlockSpec((1, batch_rows, width), lambda q, place: (q, 0, 0)),
                ),
            ),
            compiler_params=pltpu.CompilerParams(vmem_limit_bytes=24 << 20),
            cost_estimate=pl.CostEstimate(
                flops=work, bytes_accessed=8 << 20, transcendentals=0
            ),
        )(place, score_grad, score_grad, items)
    with jax.named_scope("item_grad"):
        item_got = exchange(item_send, "nx").astype(f32)
        item_got, user_keep, user_send = lax.optimization_barrier(
            (item_got, user_keep, user_send)
        )
        others = jnp.arange(nx, dtype=i32)[:, None, None] != my_x
        item_unit_grad = item_own + jnp.sum(jnp.where(others, item_got, 0.0), axis=0)
        item_vec_grad = norm_backward(item_vec, item_factor, item_unit_grad).astype(bf16)
        row_grad = contract_last(item_vec_grad, w_item).astype(bf16)
    owner_id = item_owner[0, :, 0]
    with jax.named_scope("hot_and_w"):
        w_local = contract_first(item_block, item_vec_grad)
        hot_count = hot_table.shape[0]
        hot_match = (hot_row[0][:, None] == jnp.arange(hot_count, dtype=i32)[None, :]) & (
            owner_id == owners
        )[:, None]
        hot_local = contract_first(hot_match.astype(bf16), row_grad)
        half = width // 2
        rows = hot_count + width
        core = lax.axis_index("rep")
        halves = jnp.stack(
            [
                jnp.concatenate([part[:, at * half : (at + 1) * half] for part in (hot_local, w_local)])
                for at in range(2)
            ]
        )
        chip = lax.dynamic_index_in_dim(halves, core, 0, keepdims=False) + shift(
            lax.dynamic_index_in_dim(halves, 1 - core, 0, keepdims=False), "rep", 1
        )
        got_one = flip(user_send, "ny", 1)
        plane = jnp.sum(
            exchange(chip.reshape(nx * ny, rows // (nx * ny), half), ("nx", "ny")), axis=0
        )
        plane_high = lax.reduce_precision(plane, exponent_bits=8, mantissa_bits=7)
        plane_rows = jnp.concatenate([plane_high, plane - plane_high], axis=1).astype(bf16)
        plane_rows, got_one = lax.optimization_barrier((plane_rows, got_one))
        user_sums = user_keep + got_one.astype(f32)
        got_two = flip(user_sums[1::2].astype(bf16), "ny", 2)
    with jax.named_scope("cold"):
        owner_hits = (owner_id[:, None] == jnp.arange(owners, dtype=i32)[None, :]).astype(bf16)
        place = jnp.arange(batch_rows, dtype=i32)
        earlier = (place[:, None] > place[None, :]).astype(bf16)
        before = jnp.dot(earlier, owner_hits, preferred_element_type=f32)
        slot = jnp.sum(before * owner_hits.astype(f32), axis=1).astype(i32)
        target = jnp.where(owner_id < owners, owner_id * SLOTS + slot, -1)
        placed = (
            jnp.arange(owners * SLOTS, dtype=i32)[:, None] == target[None, :]
        ).astype(bf16)
        mark = cold_offset[0] + 1
        slot_hits = (slot[:, None] == jnp.arange(SLOTS, dtype=i32)[None, :]).astype(bf16)
        high = contract_first(owner_hits * (mark // 256).astype(bf16)[:, None], slot_hits)
        low = contract_first(owner_hits * (mark % 256).astype(bf16)[:, None], slot_hits)
        marks = jnp.concatenate([high, low], axis=1).astype(bf16)
        marks = jnp.pad(marks[:, None, :], ((0, 0), (0, SLOTS - CAP - 1), (0, width - 2 * SLOTS)))
        send_rows = jnp.dot(placed, row_grad, preferred_element_type=f32).astype(bf16)
        send_rows = send_rows.reshape(owners, SLOTS, width)[:, :CAP]
        to_all = jnp.broadcast_to(plane_rows[None], (owners,) + plane_rows.shape)
        got = exchange(jnp.concatenate([send_rows, marks, to_all], axis=1), "own")
        got, got_two = lax.optimization_barrier((got, got_two))
        user_sums = user_sums[0::2] + got_two.astype(f32)
        got_three = flip(user_sums[1].astype(bf16), "ny", 4)
        got_marks = got[:, CAP].astype(f32)
        offsets = (got_marks[:, :SLOTS] * 256.0 + got_marks[:, SLOTS : 2 * SLOTS]).astype(i32) - 1
        local_rows = cold_table.shape[1]
        lands = (
            jnp.arange(local_rows, dtype=i32)[:, None] == offsets.reshape(-1)[None, :]
        ).astype(bf16)
        cold_grad = jnp.dot(
            lands, got[:, :SLOTS].reshape(owners * SLOTS, width), preferred_element_type=f32
        )
        cold_table_new, cold_accum_new = adagrad(cold_table[0], cold_accum[0], cold_grad)
    with jax.named_scope("hot_and_w_back"):
        got_plane = got[:, SLOTS:].astype(f32)
        total = jnp.sum(got_plane[:, :, :half] + got_plane[:, :, half:], axis=0)
        mine = spread(total, ("nx", "ny")).reshape(rows, half)
        mine, got_three, cold_table_new, cold_accum_new = lax.optimization_barrier(
            (mine, got_three, cold_table_new, cold_accum_new)
        )
        other = shift(mine, "rep", 1)
        summed = jnp.concatenate(
            [jnp.where(core == 0, mine, other), jnp.where(core == 0, other, mine)], axis=1
        )
        hot_table_new, hot_accum_new = adagrad(hot_table, hot_accum, summed[:hot_count])
        w_grad = summed[hot_count:]
    with jax.named_scope("user_grad"):
        user_unit_grad = user_sums[0] + got_three.astype(f32)
        user_grad = norm_backward(user_float, user_factor, user_unit_grad).astype(bf16)
    return (
        user_grad[None],
        w_grad,
        hot_table_new,
        hot_accum_new,
        cold_table_new[None],
        cold_accum_new[None],
    )


def solution(mesh):
    owners, neg, rep = (mesh.shape[name] for name in ("own", "neg", "rep"))
    grid = Mesh(
        mesh.devices.reshape(owners, NX, neg // NX, rep), ("own", "nx", "ny", "rep")
    )
    group, pairs, blocks = ("own", "rep"), ("nx", "ny"), ("nx", "ny", "rep")
    return jax.shard_map(
        on_device,
        mesh=grid,
        in_specs=(
            P(group, pairs, None),
            P(group, pairs, None),
            P(),
            P(group, pairs),
            P(group, pairs, None),
            P(group, pairs),
            P(group, pairs),
            P(),
            P(),
            P("own", blocks, None),
            P("own", blocks, None),
        ),
        out_specs=(
            P(group, pairs, None),
            P(),
            P(),
            P(),
            P("own", blocks, None),
            P("own", blocks, None),
        ),
        check_vma=False,
    )
```

```python
import functools

import jax
import jax.numpy as jnp
from jax import lax
from jax.experimental import pallas as pl
from jax.experimental.pallas import tpu as pltpu
from jax.sharding import Mesh, PartitionSpec as P

CAP = 56
NX = 4
SLOTS = 64
PAD = 16

score_scale = 20.0
learn_rate = 0.1
norm_eps = 1e-06

bf16 = jnp.bfloat16
f32 = jnp.float32
i32 = jnp.int32


def normalize(values):
    factor = lax.rsqrt(jnp.sum(values * values, axis=-1, keepdims=True) + norm_eps)
    return (values * factor, factor)


def norm_backward(values, factor, upstream):
    inner = jnp.sum(values * upstream, axis=-1, keepdims=True)
    return factor * upstream - factor * factor * factor * values * inner


def adagrad(table, accum, grads):
    accum_new = accum + grads * grads
    return (table - learn_rate * grads * lax.rsqrt(accum_new), accum_new)


def contract_first(left, right):
    return lax.dot_general(
        left, right, (((0,), (0,)), ((), ())), preferred_element_type=f32
    )


def contract_last(left, right):
    return lax.dot_general(
        left, right, (((1,), (1,)), ((), ())), preferred_element_type=f32
    )


def exchange(blocks, axis):
    return lax.all_to_all(blocks, axis, split_axis=0, concat_axis=0, tiled=True)


def spread(block, axis):
    count = lax.axis_size(axis)
    return exchange(jnp.broadcast_to(block[None], (count,) + block.shape), axis)


def shift(block, axis, step):
    count = lax.axis_size(axis)
    return lax.ppermute(block, axis, [(i, (i + step) % count) for i in range(count)])


def flip(block, axis, mask):
    count = lax.axis_size(axis)
    return lax.ppermute(block, axis, [(i, i ^ mask) for i in range(count)])


def unpack(packed, items, log_counts):
    rows = packed[0].shape[0] - PAD
    for at, ref in enumerate(packed):
        items[pl.ds(at * rows, rows), :] = ref[:rows, :]
        tail = ref[rows:, :].astype(f32)
        logs = jnp.log(tail[:1] * 256.0 + tail[1:2])
        log_counts[pl.ds(at * rows, rows), :] = jnp.broadcast_to(logs, (128, rows)).T


def scores_of(items, log_counts, users):
    logs = jnp.tile(log_counts[...], (1, users.shape[0] // 128))
    return jnp.exp(score_scale * contract_last(items[...], users) - logs)


def sums_kernel(*refs):
    users, packed, (sums, items, log_counts) = refs[0], refs[1:-3], refs[-3:]
    unpack(packed, items, log_counts)
    tiles, tile = sums.shape[1], sums.shape[2]
    for t in range(tiles):
        values = scores_of(items, log_counts, users[t * tile : (t + 1) * tile, :])
        part = jnp.sum(values, axis=0, keepdims=True)
        for at in range(sums.shape[0]):
            sums[at, t : t + 1, :] = part


def grads_kernel(
    place, users, sums, items, log_counts, score_grad, item_send, item_own, total
):
    t = pl.program_id(0)
    tile = users.shape[0]
    square = (tile, tile)
    eye = lax.broadcasted_iota(i32, square, 0) == lax.broadcasted_iota(i32, square, 1)
    inverse = 1.0 / jnp.sum(sums[:, pl.ds(t, 1), :], axis=0)
    values = scores_of(items, log_counts, users[...]) * inverse
    own = jnp.where(eye & (place[1] == t), values[:tile] - 1.0, values[:tile])
    score_grad[:tile, :] = own.astype(bf16)
    score_grad[tile:, :] = values[tile:].astype(bf16)
    part = jnp.dot(score_grad[...], users[...], preferred_element_type=f32)

    @pl.when(t == 0)
    def _():
        total[...] = part

    @pl.when(t > 0)
    def _():
        total[...] += part

    @pl.when(t == pl.num_programs(0) - 1)
    def _():
        count, rows = item_send.shape[0], item_send.shape[1]
        item_own[...] = score_scale * total[:rows, :]
        for k in range(count):
            item_send[lax.rem(place[0] + (count - k), count)] = (
                score_scale * total[k * rows : (k + 1) * rows, :]
            ).astype(bf16)


def users_kernel(place, even, odd, items, keep, send):
    keep[0, 0] = score_scale * contract_first(even[...], items[...])
    send[0, 0] = (score_scale * contract_first(odd[...], items[...])).astype(bf16)


def kernel_call(body, outs, scratch, flops):
    whole = pl.BlockSpec(memory_space=pltpu.VMEM)
    return functools.partial(
        pl.pallas_call,
        body,
        out_shape=outs,
        out_specs=jax.tree.map(lambda _: whole, outs),
        scratch_shapes=scratch,
        compiler_params=pltpu.CompilerParams(vmem_limit_bytes=24 << 20),
        cost_estimate=pl.CostEstimate(flops=flops, bytes_accessed=4 << 20, transcendentals=2 << 20),
    )


def on_device(
    user_vec,
    item_rows,
    w_item,
    item_count,
    item_owner,
    hot_row,
    cold_offset,
    hot_table,
    hot_accum,
    cold_table,
    cold_accum,
):
    owners = lax.axis_size("own")
    ny = lax.axis_size("ny")
    nx = lax.axis_size("nx")
    user_float = user_vec[0].astype(f32)
    item_block = item_rows[0]
    batch_rows, width = item_block.shape
    with jax.named_scope("users_along_y"):
        user_norm, user_factor = normalize(user_float)
        user_unit = user_norm.astype(bf16)
        users = spread(user_unit, "ny").reshape(ny * batch_rows, width)
    with jax.named_scope("items_along_x"):
        item_vec = jnp.dot(item_block, w_item, preferred_element_type=f32)
        item_norm, item_factor = normalize(item_vec)
        item_unit = item_norm.astype(bf16)
        counts = item_count[0]
        count_rows = jnp.stack([counts // 256, counts % 256]).astype(bf16)
        packed = jnp.concatenate(
            [item_unit, jnp.pad(count_rows, ((0, PAD - 2), (0, 0)))], axis=0
        )
        blocks = [packed] + [shift(packed, "nx", k) for k in range(1, nx)]
    pairs = (nx * batch_rows, width)
    whole = pl.BlockSpec(memory_space=pltpu.VMEM)
    work = 2 * nx * ny * batch_rows * batch_rows * width
    my_x, my_y = lax.axis_index("nx"), lax.axis_index("ny")
    with jax.named_scope("sums_along_y"):
        part_sums, items, log_counts = kernel_call(
            sums_kernel,
            (
                jax.ShapeDtypeStruct((ny, ny, batch_rows), f32),
                jax.ShapeDtypeStruct(pairs, bf16),
                jax.ShapeDtypeStruct((pairs[0], 128), f32),
            ),
            [],
            work,
        )(in_specs=[whole] * (1 + nx))(users, *blocks)
        sums = exchange(part_sums, "ny")
    with jax.named_scope("score_grad"):
        place = jnp.stack([my_x, my_y]).astype(i32)
        fixed = lambda shape: pl.BlockSpec(shape, lambda t, place: (0,) * len(shape))
        sent = (nx, batch_rows, width)
        score_grad, item_send, item_own = pl.pallas_call(
            grads_kernel,
            out_shape=(
                pltpu.HBM((pairs[0], ny * batch_rows), bf16),
                jax.ShapeDtypeStruct(sent, bf16),
                jax.ShapeDtypeStruct((batch_rows, width), f32),
            ),
            grid_spec=pltpu.PrefetchScalarGridSpec(
                num_scalar_prefetch=1,
                grid=(ny,),
                in_specs=[
                    pl.BlockSpec((batch_rows, width), lambda t, place: (t, 0)),
                    fixed(sums.shape),
                    fixed(pairs),
                    fixed((pairs[0], 128)),
                ],
                out_specs=(
                    pl.BlockSpec((pairs[0], batch_rows), lambda t, place: (0, t)),
                    fixed(sent),
                    fixed((batch_rows, width)),
                ),
                scratch_shapes=[pltpu.VMEM(pairs, f32)],
            ),
            compiler_params=pltpu.CompilerParams(vmem_limit_bytes=24 << 20),
            cost_estimate=pl.CostEstimate(
                flops=2 * work, bytes_accessed=8 << 20, transcendentals=2 << 20
            ),
        )(place, users, sums, items, log_counts)
    with jax.named_scope("user_part"):
        user_keep, user_send = pl.pallas_call(
            users_kernel,
            out_shape=(
                jax.ShapeDtypeStruct((2, ny // 4, batch_rows, width), f32),
                jax.ShapeDtypeStruct((2, ny // 4, batch_rows, width), bf16),
            ),
            grid_spec=pltpu.PrefetchScalarGridSpec(
                num_scalar_prefetch=1,
                grid=(ny // 2,),
                in_specs=[
                    pl.BlockSpec(
                        (pairs[0], batch_rows),
                        lambda q, place: (0, lax.bitwise_xor(2 * q, place[1])),
                    ),
                    pl.BlockSpec(
                        (pairs[0], batch_rows),
                        lambda q, place: (0, lax.bitwise_xor(2 * q + 1, place[1])),
                    ),
                    fixed(pairs),
                ],
                out_specs=(
                    pl.BlockSpec((1, 1, batch_rows, width), lambda q, place: (q % 2, q // 2, 0, 0)),
                    pl.BlockSpec((1, 1, batch_rows, width), lambda q, place: (q % 2, q // 2, 0, 0)),
                ),
            ),
            compiler_params=pltpu.CompilerParams(vmem_limit_bytes=24 << 20),
            cost_estimate=pl.CostEstimate(
                flops=work, bytes_accessed=8 << 20, transcendentals=0
            ),
        )(place, score_grad, score_grad, items)
    with jax.named_scope("item_grad"):
        item_got = exchange(item_send, "nx").astype(f32)
        item_got, user_keep, user_send = lax.optimization_barrier(
            (item_got, user_keep, user_send)
        )
        others = jnp.arange(nx, dtype=i32)[:, None, None] != my_x
        item_unit_grad = item_own + jnp.sum(jnp.where(others, item_got, 0.0), axis=0)
        item_vec_grad = norm_backward(item_vec, item_factor, item_unit_grad).astype(bf16)
        row_grad = contract_last(item_vec_grad, w_item).astype(bf16)
    owner_id = item_owner[0, :, 0]
    with jax.named_scope("hot_and_w"):
        w_local = contract_first(item_block, item_vec_grad)
        hot_count = hot_table.shape[0]
        hot_match = (hot_row[0][:, None] == jnp.arange(hot_count, dtype=i32)[None, :]) & (
            owner_id == owners
        )[:, None]
        hot_local = contract_first(hot_match.astype(bf16), row_grad)
        half = width // 2
        rows = hot_count + width
        core = lax.axis_index("rep")
        halves = jnp.stack(
            [
                jnp.concatenate([part[:, at * half : (at + 1) * half] for part in (hot_local, w_local)])
                for at in range(2)
            ]
        )
        chip = lax.dynamic_index_in_dim(halves, core, 0, keepdims=False) + shift(
            lax.dynamic_index_in_dim(halves, 1 - core, 0, keepdims=False), "rep", 1
        )
        got_first = flip(user_send[1], "ny", 1)
        plane = jnp.sum(
            exchange(chip.reshape(nx * ny, rows // (nx * ny), half), ("nx", "ny")), axis=0
        )
        plane_high = lax.reduce_precision(plane, exponent_bits=8, mantissa_bits=7)
        plane_rows = jnp.concatenate([plane_high, plane - plane_high], axis=1).astype(bf16)
        plane_rows, got_first, user_rest = lax.optimization_barrier(
            (plane_rows, got_first, user_send[0])
        )
        got_two = flip((user_keep[1] + got_first.astype(f32)).astype(bf16), "ny", 2)
        got_rest = flip(user_rest, "ny", 1)
    with jax.named_scope("cold"):
        owner_hits = (owner_id[:, None] == jnp.arange(owners, dtype=i32)[None, :]).astype(bf16)
        place = jnp.arange(batch_rows, dtype=i32)
        earlier = (place[:, None] > place[None, :]).astype(bf16)
        before = jnp.dot(earlier, owner_hits, preferred_element_type=f32)
        slot = jnp.sum(before * owner_hits.astype(f32), axis=1).astype(i32)
        target = jnp.where(owner_id < owners, owner_id * SLOTS + slot, -1)
        placed = (
            jnp.arange(owners * SLOTS, dtype=i32)[:, None] == target[None, :]
        ).astype(bf16)
        mark = cold_offset[0] + 1
        slot_hits = (slot[:, None] == jnp.arange(SLOTS, dtype=i32)[None, :]).astype(bf16)
        high = contract_first(owner_hits * (mark // 256).astype(bf16)[:, None], slot_hits)
        low = contract_first(owner_hits * (mark % 256).astype(bf16)[:, None], slot_hits)
        marks = jnp.concatenate([high, low], axis=1).astype(bf16)
        marks = jnp.pad(marks[:, None, :], ((0, 0), (0, SLOTS - CAP - 1), (0, width - 2 * SLOTS)))
        send_rows = jnp.dot(placed, row_grad, preferred_element_type=f32).astype(bf16)
        send_rows = send_rows.reshape(owners, SLOTS, width)[:, :CAP]
        to_all = jnp.broadcast_to(plane_rows[None], (owners,) + plane_rows.shape)
        got = exchange(jnp.concatenate([send_rows, marks, to_all], axis=1), "own")
        got, got_two, got_rest = lax.optimization_barrier((got, got_two, got_rest))
        user_sums = user_keep[0] + got_rest.astype(f32) + got_two.astype(f32)
        got_three = flip(user_sums[1].astype(bf16), "ny", 4)
        got_marks = got[:, CAP].astype(f32)
        offsets = (got_marks[:, :SLOTS] * 256.0 + got_marks[:, SLOTS : 2 * SLOTS]).astype(i32) - 1
        local_rows = cold_table.shape[1]
        lands = (
            jnp.arange(local_rows, dtype=i32)[:, None] == offsets.reshape(-1)[None, :]
        ).astype(bf16)
        cold_grad = jnp.dot(
            lands, got[:, :SLOTS].reshape(owners * SLOTS, width), preferred_element_type=f32
        )
        cold_table_new, cold_accum_new = adagrad(cold_table[0], cold_accum[0], cold_grad)
    with jax.named_scope("hot_and_w_back"):
        got_plane = got[:, SLOTS:].astype(f32)
        total = jnp.sum(got_plane[:, :, :half] + got_plane[:, :, half:], axis=0)
        mine = spread(total, ("nx", "ny")).reshape(rows, half)
        mine, got_three, cold_table_new, cold_accum_new = lax.optimization_barrier(
            (mine, got_three, cold_table_new, cold_accum_new)
        )
        other = shift(mine, "rep", 1)
        summed = jnp.concatenate(
            [jnp.where(core == 0, mine, other), jnp.where(core == 0, other, mine)], axis=1
        )
        hot_table_new, hot_accum_new = adagrad(hot_table, hot_accum, summed[:hot_count])
        w_grad = summed[hot_count:]
    with jax.named_scope("user_grad"):
        user_unit_grad = user_sums[0] + got_three.astype(f32)
        user_grad = norm_backward(user_float, user_factor, user_unit_grad).astype(bf16)
    return (
        user_grad[None],
        w_grad,
        hot_table_new,
        hot_accum_new,
        cold_table_new[None],
        cold_accum_new[None],
    )


def solution(mesh):
    owners, neg, rep = (mesh.shape[name] for name in ("own", "neg", "rep"))
    grid = Mesh(
        mesh.devices.reshape(owners, NX, neg // NX, rep), ("own", "nx", "ny", "rep")
    )
    group, pairs, blocks = ("own", "rep"), ("nx", "ny"), ("nx", "ny", "rep")
    return jax.shard_map(
        on_device,
        mesh=grid,
        in_specs=(
            P(group, pairs, None),
            P(group, pairs, None),
            P(),
            P(group, pairs),
            P(group, pairs, None),
            P(group, pairs),
            P(group, pairs),
            P(),
            P(),
            P("own", blocks, None),
            P("own", blocks, None),
        ),
        out_specs=(
            P(group, pairs, None),
            P(),
            P(),
            P(),
            P("own", blocks, None),
            P("own", blocks, None),
        ),
        check_vma=False,
    )
```
